128 devices in a mesh: qa: 8 (over x, y_lo), qb: 16 (over z, y_hi, core).
Axes of the slice: x: 4, y: 4 (y_hi: 2, y_lo: 2; y = y_hi * 2 + y_lo), z: 4, core: 2. Of those that a mesh axis runs over, the one named last changes fastest.
Arguments:
- state: float32 [2, 67108864], P(None, ('qa', 'qb')), may hold values from -6 to 6
- gates: float32 [3, 2, 2, 64, 64], replicated, may hold values from -0.5 to 0.5
Outputs:
- final_state: float32 [2, 67108864], P(None, ('qa', 'qb'))
The draws below stay inside these ranges and needn't reach their ends.
All inputs are finite; a program needn't handle non-finite values.
Results may differ from the reference program's by a relative error of at most 0.0001.
Values sent between devices are 32-bit elements; how exact they have to be, the bound alone decides.
A program may use at most 64 MiB of HBM per device.

```python
import jax
import jax.numpy as jnp
from jax import lax

LOCAL = 19
GDIM = 64
LAYERS = 3
AMPS = 67108864
N_QA = 8
N_QB = 16
DEVICES = 128


def steps_of(stream_key, extent, shards, least, high):
    def one(position, shards_of):
        steps = jax.random.uniform(jax.random.fold_in(jax.random.fold_in(stream_key, 6), position), (shards_of,), jnp.float32, least / len(shards), high / len(shards))
        return jnp.repeat(jnp.exp(steps), extent[position] // shards_of).reshape((-1,) + (1,) * (len(extent) - position - 1))

    level = one(*shards[0])
    for cut in shards[1:]:
        level = level * one(*cut)
    return level


def centred(stream_key, shape, deviation, bound, cuts=(), held_as=jnp.bfloat16):
    loudness = steps_of(stream_key, shape, cuts, -0.22, 0.18) if cuts else 1.0
    entries = jax.random.normal(stream_key, shape, jnp.float32) * deviation * loudness
    return jnp.minimum(jnp.maximum(entries, -bound), bound).astype(held_as)


def setup_inputs(seed: int = 0) -> dict:
    streams_of = jax.random.split(jax.random.key(seed), 3)
    return {
        "state": centred(streams_of[0], (2, AMPS), 1.0, 6.0, ((1, 128),), jnp.float32),
        "gates": centred(streams_of[1], (LAYERS, 2, 2, GDIM, GDIM), (2 * GDIM) ** -0.5, 0.5, (), jnp.float32),
    }


def local_order(layer, count_bits):
    span = count_bits - 7
    order = list(range(7))
    for j in range(7, count_bits):
        shifted = (j - 7 + 3 + 5 * layer) % span
        if layer % 2 == 0:
            order.append(7 + shifted)
        else:
            order.append(7 + span - 1 - shifted)
    return order


def reorder(block, layer):
    length = block.shape[1]
    count_bits = length.bit_length() - 1
    span = count_bits - 7
    order = local_order(layer, count_bits)
    shaped = block.reshape((2,) + (2,) * span + (128,))
    perm = [0] + [count_bits - order[count_bits - place] for place in range(1, span + 1)] + [span + 1]
    return jnp.transpose(shaped, perm).reshape(2, length)


def complex_apply(real_gate, imag_gate, real_in, imag_in, form):
    highest = lax.Precision.HIGHEST
    real_out = jnp.einsum(form, real_gate, real_in, precision=highest) - jnp.einsum(form, imag_gate, imag_in, precision=highest)
    imag_out = jnp.einsum(form, real_gate, imag_in, precision=highest) + jnp.einsum(form, imag_gate, real_in, precision=highest)
    return real_out, imag_out


def apply_gates(block, layer_gates):
    length = block.shape[1]
    cube = block.reshape(2, 64, 64, length // 4096)
    real_in, imag_in = complex_apply(layer_gates[0, 0], layer_gates[0, 1], cube[0], cube[1], "ab,cbl->cal")
    real_in, imag_in = complex_apply(layer_gates[1, 0], layer_gates[1, 1], real_in, imag_in, "ab,bcl->acl")
    return jnp.stack([real_in, imag_in]).reshape(2, length)


def reference(state, gates):
    share = 2 ** LOCAL
    blocks = jnp.swapaxes(state.reshape(2, DEVICES, share), 0, 1)
    high_bit = N_QB.bit_length() - 2
    for layer in range(LAYERS):
        layer_gates = gates[layer]
        blocks = lax.map(lambda block: apply_gates(reorder(block, layer), layer_gates), blocks)
        if layer % 2 == 0:
            split = blocks.reshape(DEVICES, 2, DEVICES, share // DEVICES)
            blocks = jnp.transpose(split, (2, 1, 0, 3)).reshape(DEVICES, 2, share)
        else:
            upper = 2 ** high_bit
            split = blocks.reshape(N_QA, 2, N_QB // (2 * upper), upper, 2, 2, share // 2)
            blocks = jnp.swapaxes(split, 1, 5).reshape(DEVICES, 2, share)
    return jnp.swapaxes(blocks, 0, 1).reshape(2, DEVICES * share)
```

```python
import functools

import jax
import jax.numpy as jnp
from jax import lax
from jax.experimental import pallas as pl
from jax.experimental.pallas import tpu as pltpu
from jax.sharding import PartitionSpec as P

MESH = pl.DeviceIdType.MESH
STRIDE = 53
CHUNK = 32
HALF = 128 * CHUNK


def place():
    qa, qb = lax.axis_index("qa"), lax.axis_index("qb")
    return qa // 2, (qb // 2) % 2 * 2 + qa % 2, qb // 4, qb % 2


def partner(here, step):
    x, y, z, c = here
    x = (x + step // 32) % 4
    y = (y + step // 8 % 4) % 4
    z = (z + step // 2 % 4) % 4
    c = (c + step % 2) % 2
    return x * 2 + y % 2, z * 4 + y // 2 * 2 + c


def reversed_bits(p):
    out = p % 2
    for b in range(1, 7):
        out = out * 2 + p // (1 << b) % 2
    return out


def trade(first, second, lane_bit):
    apart = 1 << lane_bit
    lane = lax.broadcasted_iota(jnp.int32, first.shape, first.ndim - 1)
    low = lane // apart % 2 == 0
    back = pltpu.roll(first, 128 - apart, first.ndim - 1)
    forth = pltpu.roll(second, apart, second.ndim - 1)
    return jnp.where(low, first, forth), jnp.where(low, back, second)


def halves(x):
    high = x.astype(jnp.bfloat16)
    return high, (x - high.astype(jnp.float32)).astype(jnp.bfloat16)


def apply(weights, x):
    both = jnp.concatenate(halves(x), axis=0)
    out = jnp.dot(weights, both, preferred_element_type=jnp.float32)
    return out[:128] + out[128:]


def one_hot(wanted):
    column = lax.broadcasted_iota(jnp.int32, (128, 128), 1)
    return (column == wanted).astype(jnp.bfloat16)


def exactly(a, b, dims):
    return lax.dot_general(a, b, (dims, ((), ())), preferred_element_type=jnp.float32).astype(
        jnp.bfloat16
    )


def prepare(gates, weights):
    row = lax.broadcasted_iota(jnp.int32, (128, 128), 0)
    low = row % 2 * 8 + row // 2 % 2 * 4 + row // 4 % 2 * 2 + row // 8 % 2
    turn = one_hot(row // 16 * 16 + low)
    natural = one_hot(row % 2 * 64 + row // 2 % 8 * 8 + row // 16)
    for layer in range(3):
        for gate in range(2):
            real, imag = gates[layer, gate, 0], gates[layer, gate, 1]
            whole = jnp.concatenate(
                [
                    jnp.concatenate([real, -imag], axis=1),
                    jnp.concatenate([imag, real], axis=1),
                ],
                axis=0,
            )
            parts = halves(whole)
            if (layer, gate) == (0, 0):
                parts = [exactly(turn, part, ((1,), (0,))) for part in parts]
            if (layer, gate) == (0, 1):
                parts = [exactly(natural, part, ((1,), (0,))) for part in parts]
                parts = [exactly(part, natural, ((1,), (1,))) for part in parts]
            high, low_part = parts
            weights[2 * layer + gate, :128] = jnp.concatenate([high, high], axis=1)
            weights[2 * layer + gate, 128:] = jnp.concatenate([low_part, low_part], axis=1)


def first_layer(x, y, out, weights):
    def second_gate(i, _):
        m = i * 2
        parts = [x[h, pl.ds(m * 16, 32)] for h in range(8)]
        a = jnp.concatenate([p[:16] for p in parts], axis=0)
        b = jnp.concatenate([p[16:] for p in parts], axis=0)
        r = apply(weights[1], jnp.concatenate([a, b], axis=1))
        y[pl.ds(m, 128, stride=64)] = r[:, :128]
        y[pl.ds(m + 1, 128, stride=64)] = r[:, 128:]
        return 0

    lax.fori_loop(0, 32, second_gate, 0, unroll=4)

    def first_gate(q, _):
        a = y[pl.ds(q * 128, 128)]
        b = y[pl.ds(q * 128 + 4096, 128)]
        r = apply(weights[0], jnp.concatenate([a, b], axis=1))
        a = r[:, :128].reshape(4, 2, 16, 128)
        b = r[:, 128:].reshape(4, 2, 16, 128)
        a0, b0 = trade(a[:, 0], b[:, 0], 6)
        a1, b1 = trade(a[:, 1], b[:, 1], 6)
        for six, pair in enumerate(((a0, a1), (b0, b1))):
            for five, value in enumerate(trade(*pair, 5)):
                for s in range(2):
                    for fifteen in range(2):
                        to = ((q % 8) * 4 + q // 8) * 4 + fifteen * 2 + six
                        out[five, pl.ds(to * CHUNK + s * 16, 16)] = value[s * 2 + fifteen]
        return 0

    lax.fori_loop(0, 32, first_gate, 0, unroll=4)


def later_layers(x, t, u, out, weights):
    def put(ref, base, r):
        for s in range(2):
            ref[pl.ds(base + s * 2048, 64, stride=32)] = r[s * 64 : s * 64 + 64]

    def gate_10(i, _):
        cols = []
        for k in range(2):
            v = x[pl.ds((i * 2 + k) * 128, 128)].reshape(4, 2, 16, 128)
            cols.append(jnp.concatenate([v[:, s].reshape(64, 128) for s in range(2)], axis=0))
        r = apply(weights[2], jnp.concatenate(cols, axis=1))
        for k in range(2):
            put(t, i * 2 + k, r[:, k * 128 : k * 128 + 128])
        return 0

    lax.fori_loop(0, 16, gate_10, 0, unroll=4)

    def gate_11(i, _):
        cols = []
        for k in range(2):
            rows = []
            for s in range(2):
                v = t[pl.ds(s * 2048 + (i * 2 + k) * 64, 64)]
                rows.extend(trade(v[:32], v[32:], 5))
            cols.append(jnp.concatenate(rows, axis=0))
        r = apply(weights[3], jnp.concatenate(cols, axis=1))
        for k in range(2):
            put(u, i * 2 + k, r[:, k * 128 : k * 128 + 128])
        return 0

    lax.fori_loop(0, 16, gate_11, 0, unroll=4)

    def gate_20(i, _):
        cols = []
        for k in range(2):
            rows = [u[pl.ds(s * 2048 + (i * 2 + k) * 64, 64)] for s in range(2)]
            cols.append(jnp.concatenate(rows, axis=0))
        r = apply(weights[4], jnp.concatenate(cols, axis=1))
        for k in range(2):
            put(t, i * 2 + k, r[:, k * 128 : k * 128 + 128])
        return 0

    lax.fori_loop(0, 16, gate_20, 0, unroll=4)

    def gate_21(i, _):
        cols = []
        for k in range(2):
            rows = []
            base = (i // 8 * 32 + i % 8 * 2 + k) * 32
            for s in range(2):
                v0 = t[pl.ds(s * 2048 + base, 32)]
                v1 = t[pl.ds(s * 2048 + base + 512, 32)]
                a0, b0 = trade(v0[:16], v0[16:], 6)
                a1, b1 = trade(v1[:16], v1[16:], 6)
                c0, c1 = trade(a0, a1, 5)
                d0, d1 = trade(b0, b1, 5)
                rows.extend([c0, d0, c1, d1])
            cols.append(jnp.concatenate(rows, axis=0))
        r = apply(weights[5], jnp.concatenate(cols, axis=1))
        for k in range(2):
            for s in range(2):
                base = i // 8 * 2048 + (i % 8 * 2 + k) * 2 + s
                out[pl.ds(base, 64, stride=32)] = r[s * 64 : s * 64 + 64, k * 128 : k * 128 + 128]
        return 0

    lax.fori_loop(0, 16, gate_21, 0, unroll=4)


def evolve(
    x_hbm, gates, landed, x, y, sent, got, t, u, ready, weights,
    load_sem, own_sems, send_sems, recv_sems,
):
    here = place()
    me = lax.axis_index("qa") * 16 + lax.axis_index("qb")
    load = pltpu.make_async_copy(x_hbm, x, load_sem)
    load.start()
    barrier = pltpu.get_barrier_semaphore()

    def greet(k, _):
        pl.semaphore_signal(barrier, inc=1, device_id=partner(here, k), device_id_type=MESH)
        return 0

    lax.fori_loop(1, 128, greet, 0)
    prepare(gates, weights)
    load.wait()
    first_layer(x, y, sent, weights)
    pl.semaphore_wait(barrier, 127)

    def spread(source, target, chunk_of, slot, number):
        send, recv = send_sems.at[number], recv_sems.at[number]
        own = pltpu.make_async_copy(
            source.at[pl.ds(chunk_of(me) * CHUNK, CHUNK)],
            target.at[pl.ds(slot * CHUNK, CHUNK)],
            own_sems.at[number],
        )
        own.start()

        def one(k, _):
            qa, qb = partner(here, 1 + k * STRIDE % 127)
            pltpu.make_async_remote_copy(
                src_ref=source.at[pl.ds(chunk_of(qa * 16 + qb) * CHUNK, CHUNK)],
                dst_ref=target.at[pl.ds(slot * CHUNK, CHUNK)],
                send_sem=send,
                recv_sem=recv,
                device_id=(qa, qb),
                device_id_type=MESH,
            ).start()
            return 0

        lax.fori_loop(0, 127, one, 0)
        every = pltpu.make_async_remote_copy(
            src_ref=source.at[pl.ds(0, 127 * CHUNK)],
            dst_ref=target.at[pl.ds(0, 127 * CHUNK)],
            send_sem=send,
            recv_sem=recv,
            device_id=partner(here, 1),
            device_id_type=MESH,
        )
        return own, every

    mine = reversed_bits(me)
    out_first = [spread(sent.at[i], got.at[i], lambda p: p, mine, i) for i in range(2)]
    out_second = []
    for i in range(2):
        own, every = out_first[i]
        own.wait()
        every.wait_recv()
        later_layers(got.at[i], t, u, ready.at[i], weights)
        out_second.append(
            spread(ready.at[i], landed.at[i], lambda p: p % 2 * 64 + p // 2, me, 2 + i)
        )
    for _, every in out_first:
        every.wait_send()
    for own, every in out_second:
        own.wait()
        every.wait()


def finish(landed, out):
    for r in range(8):
        v = [[landed[five, r * 2 + six] for five in range(2)] for six in range(2)]
        a0, b0 = trade(v[0][0], v[1][0], 6)
        a1, b1 = trade(v[0][1], v[1][1], 6)
        for fourteen, pair in enumerate(((a0, a1), (b0, b1))):
            for twentyfour, value in enumerate(trade(*pair, 5)):
                out[0, fourteen, r, twentyfour] = value


def body(state, gates):
    rows = state.reshape(2, 4096, 128).transpose(1, 0, 2).reshape(8, 1024, 128)
    f32 = jnp.float32
    landed = pl.pallas_call(
        evolve,
        out_shape=jax.ShapeDtypeStruct((2, HALF, 128), f32),
        in_specs=[pl.BlockSpec(memory_space=pl.ANY), pl.BlockSpec(memory_space=pltpu.VMEM)],
        out_specs=pl.BlockSpec(memory_space=pl.ANY),
        scratch_shapes=[
            pltpu.VMEM((8, 1024, 128), f32),
            pltpu.VMEM((8192, 128), f32),
            pltpu.VMEM((2, HALF, 128), f32),
            pltpu.VMEM((2, HALF, 128), f32),
            pltpu.VMEM((HALF, 128), f32),
            pltpu.VMEM((HALF, 128), f32),
            pltpu.VMEM((2, HALF, 128), f32),
            pltpu.VMEM((6, 256, 256), jnp.bfloat16),
            pltpu.SemaphoreType.DMA,
            pltpu.SemaphoreType.DMA((4,)),
            pltpu.SemaphoreType.DMA((4,)),
            pltpu.SemaphoreType.DMA((4,)),
        ],
        compiler_params=pltpu.CompilerParams(
            collective_id=0, has_side_effects=True, vmem_limit_bytes=48 * 2**20
        ),
        name="evolve",
    )(rows, gates)
    out = pl.pallas_call(
        finish,
        grid=(8,),
        out_shape=jax.ShapeDtypeStruct((8, 2, 8, 2, 32, 128), f32),
        in_specs=[pl.BlockSpec((2, 16, CHUNK, 128), lambda i: (0, i, 0, 0))],
        out_specs=pl.BlockSpec((1, 2, 8, 2, 32, 128), lambda i: (i, 0, 0, 0, 0, 0)),
        compiler_params=pltpu.CompilerParams(vmem_limit_bytes=16 * 2**20),
        name="finish",
    )(landed.reshape(2, 128, CHUNK, 128))
    return out.reshape(4096, 2, 128).transpose(1, 0, 2).reshape(2, -1)


def solution(mesh):
    placed = (P(None, ("qa", "qb")), P())
    return jax.shard_map(
        body, mesh=mesh, in_specs=placed, out_specs=P(None, ("qa", "qb")), check_vma=False
    )
```

```python
import functools

import jax
import jax.numpy as jnp
from jax import lax
from jax.experimental import pallas as pl
from jax.experimental.pallas import tpu as pltpu
from jax.sharding import PartitionSpec as P

MESH = pl.DeviceIdType.MESH
STRIDE = 116
CHUNK = 32
HALF = 128 * CHUNK


def place():
    qa, qb = lax.axis_index("qa"), lax.axis_index("qb")
    return qa // 2, (qb // 2) % 2 * 2 + qa % 2, qb // 4, qb % 2


def partner(here, step):
    x, y, z, c = here
    x = (x + step // 32) % 4
    y = (y + step // 8 % 4) % 4
    z = (z + step // 2 % 4) % 4
    c = (c + step % 2) % 2
    return x * 2 + y % 2, z * 4 + y // 2 * 2 + c


def reversed_bits(p):
    out = p % 2
    for b in range(1, 7):
        out = out * 2 + p // (1 << b) % 2
    return out


def trade(first, second, lane_bit):
    apart = 1 << lane_bit
    lane = lax.broadcasted_iota(jnp.int32, first.shape, first.ndim - 1)
    low = lane // apart % 2 == 0
    back = pltpu.roll(first, 128 - apart, first.ndim - 1)
    forth = pltpu.roll(second, apart, second.ndim - 1)
    return jnp.where(low, first, forth), jnp.where(low, back, second)


def trade_both(parts):
    lane = lax.broadcasted_iota(jnp.int32, parts[0].shape, parts[0].ndim - 1)
    odd, upper = lane // 32 % 2 == 1, lane // 64 == 1
    once = [jnp.where(odd, parts[(i + 1) % 4], parts[i]) for i in range(4)]
    skewed = [jnp.where(upper, once[(i + 2) % 4], once[i]) for i in range(4)]
    turned = skewed[:1] + [pltpu.roll(skewed[i], 32 * i, lane.ndim - 1) for i in range(1, 4)]
    once = [jnp.where(odd, turned[(i + 1) % 4], turned[i]) for i in range(4)]
    return [jnp.where(upper, once[(2 - j) % 4], once[-j % 4]) for j in range(4)]


def halves(x):
    high = x.astype(jnp.bfloat16)
    return high, (x - high.astype(jnp.float32)).astype(jnp.bfloat16)


def apply(weights, x):
    both = jnp.concatenate(halves(x), axis=0)
    out = jnp.dot(weights, both, preferred_element_type=jnp.float32)
    return out[:128] + out[128:]


def one_hot(wanted):
    column = lax.broadcasted_iota(jnp.int32, (128, 128), 1)
    return (column == wanted).astype(jnp.bfloat16)


def exactly(a, b, dims):
    return lax.dot_general(a, b, (dims, ((), ())), preferred_element_type=jnp.float32).astype(
        jnp.bfloat16
    )


def prepare(gates, weights, layers):
    row = lax.broadcasted_iota(jnp.int32, (128, 128), 0)
    low = row % 2 * 8 + row // 2 % 2 * 4 + row // 4 % 2 * 2 + row // 8 % 2
    turn = one_hot(row // 16 * 16 + low)
    natural = one_hot(row % 2 * 64 + row // 2 % 8 * 8 + row // 16)
    for layer in layers:
        for gate in range(2):
            real, imag = gates[layer, gate, 0], gates[layer, gate, 1]
            whole = jnp.concatenate(
                [
                    jnp.concatenate([real, -imag], axis=1),
                    jnp.concatenate([imag, real], axis=1),
                ],
                axis=0,
            )
            parts = halves(whole)
            if (layer, gate) == (0, 0):
                parts = [exactly(turn, part, ((1,), (0,))) for part in parts]
            if (layer, gate) == (0, 1):
                parts = [exactly(natural, part, ((1,), (0,))) for part in parts]
                parts = [exactly(part, natural, ((1,), (1,))) for part in parts]
            high, low_part = parts
            weights[2 * layer + gate, :128] = jnp.concatenate([high, high], axis=1)
            weights[2 * layer + gate, 128:] = jnp.concatenate([low_part, low_part], axis=1)


def first_layer(x, y, out, weights, greet):
    def second_gate(i, _):
        m = i * 2
        parts = [x[h, pl.ds(m * 16, 32)] for h in range(8)]
        a = jnp.concatenate([p[:16] for p in parts], axis=0)
        b = jnp.concatenate([p[16:] for p in parts], axis=0)
        r = apply(weights[1], jnp.concatenate([a, b], axis=1))
        y[pl.ds(m, 128, stride=64)] = r[:, :128]
        y[pl.ds(m + 1, 128, stride=64)] = r[:, 128:]
        return 0

    lax.fori_loop(0, 32, second_gate, 0, unroll=8)

    def first_gate(q, _):
        a = y[pl.ds(q * 128, 128)]
        b = y[pl.ds(q * 128 + 4096, 128)]
        r = apply(weights[0], jnp.concatenate([a, b], axis=1))
        a = r[:, :128].reshape(4, 2, 16, 128)
        b = r[:, 128:].reshape(4, 2, 16, 128)
        for j, value in enumerate(trade_both([a[:, 0], a[:, 1], b[:, 0], b[:, 1]])):
            for s in range(2):
                for fifteen in range(2):
                    to = ((q % 8) * 4 + q // 8) * 4 + fifteen * 2 + j // 2
                    out[j % 2, pl.ds(to * CHUNK + s * 16, 16)] = value[s * 2 + fifteen]
        return 0

    lax.fori_loop(0, 32, first_gate, 0, unroll=8)


def later_layers(x, t, u, out, weights):
    def put(ref, base, r):
        for s in range(2):
            ref[pl.ds(base + s * 2048, 64, stride=32)] = r[s * 64 : s * 64 + 64]

    def gate_10(i, _):
        cols = []
        for k in range(2):
            v = x[pl.ds((i * 2 + k) * 128, 128)].reshape(4, 2, 16, 128)
            cols.append(jnp.concatenate([v[:, s].reshape(64, 128) for s in range(2)], axis=0))
        r = apply(weights[2], jnp.concatenate(cols, axis=1))
        for k in range(2):
            put(t, i * 2 + k, r[:, k * 128 : k * 128 + 128])
        return 0

    lax.fori_loop(0, 16, gate_10, 0, unroll=8)

    def gate_11(i, _):
        cols = []
        for k in range(2):
            rows = []
            for s in range(2):
                v = t[pl.ds(s * 2048 + (i * 2 + k) * 64, 64)]
                rows.extend(trade(v[:32], v[32:], 5))
            cols.append(jnp.concatenate(rows, axis=0))
        r = apply(weights[3], jnp.concatenate(cols, axis=1))
        for k in range(2):
            put(u, i * 2 + k, r[:, k * 128 : k * 128 + 128])
        return 0

    lax.fori_loop(0, 16, gate_11, 0, unroll=8)

    def gate_20(i, _):
        cols = []
        for k in range(2):
            rows = [u[pl.ds(s * 2048 + (i * 2 + k) * 64, 64)] for s in range(2)]
            cols.append(jnp.concatenate(rows, axis=0))
        r = apply(weights[4], jnp.concatenate(cols, axis=1))
        for k in range(2):
            put(t, i * 2 + k, r[:, k * 128 : k * 128 + 128])
        return 0

    lax.fori_loop(0, 16, gate_20, 0, unroll=8)

    def gate_21(i, _):
        cols = []
        for k in range(2):
            rows = []
            base = (i // 8 * 32 + i % 8 * 2 + k) * 32
            for s in range(2):
                v0 = t[pl.ds(s * 2048 + base, 32)]
                v1 = t[pl.ds(s * 2048 + base + 512, 32)]
                c = trade_both([v0[:16], v1[:16], v0[16:], v1[16:]])
                rows.extend([c[0], c[2], c[1], c[3]])
            cols.append(jnp.concatenate(rows, axis=0))
        r = apply(weights[5], jnp.concatenate(cols, axis=1))
        for k in range(2):
            for s in range(2):
                base = i // 8 * 2048 + (i % 8 * 2 + k) * 2 + s
                out[pl.ds(base, 64, stride=32)] = r[s * 64 : s * 64 + 64, k * 128 : k * 128 + 128]
        return 0

    lax.fori_loop(0, 16, gate_21, 0, unroll=8)


def evolve(
    x_hbm, gates_hbm, landed, x, y, sent, got, t, u, ready, gates, weights,
    load_sems, own_sems, send_sems, recv_sems,
):
    here = place()
    me = lax.axis_index("qa") * 16 + lax.axis_index("qb")
    load_gates = pltpu.make_async_copy(gates_hbm, gates, load_sems.at[0])
    load_gates.start()
    load = pltpu.make_async_copy(x_hbm, x, load_sems.at[1])
    load.start()
    barrier = pltpu.get_barrier_semaphore()

    def greet(k, _=0):
        pl.semaphore_signal(barrier, inc=1, device_id=partner(here, k), device_id_type=MESH)
        return 0

    lax.fori_loop(1, 128, greet, 0)
    load_gates.wait()
    prepare(gates, weights, (0,))
    load.wait()
    first_layer(x, y, sent, weights, greet)
    pl.semaphore_wait(barrier, 127)

    def spread(source, target, chunk_of, slot, number):
        send, recv = send_sems.at[number], recv_sems.at[number]
        own = pltpu.make_async_copy(
            source.at[pl.ds(chunk_of(me) * CHUNK, CHUNK)],
            target.at[pl.ds(slot * CHUNK, CHUNK)],
            own_sems.at[number],
        )
        own.start()

        def one(k, _):
            qa, qb = partner(here, 1 + k * STRIDE % 127)
            pltpu.make_async_remote_copy(
                src_ref=source.at[pl.ds(chunk_of(qa * 16 + qb) * CHUNK, CHUNK)],
                dst_ref=target.at[pl.ds(slot * CHUNK, CHUNK)],
                send_sem=send,
                recv_sem=recv,
                device_id=(qa, qb),
                device_id_type=MESH,
            ).start()
            return 0

        lax.fori_loop(0, 127, one, 0)
        every = pltpu.make_async_remote_copy(
            src_ref=source.at[pl.ds(0, 127 * CHUNK)],
            dst_ref=target.at[pl.ds(0, 127 * CHUNK)],
            send_sem=send,
            recv_sem=recv,
            device_id=partner(here, 1),
            device_id_type=MESH,
        )
        return own, every

    mine = reversed_bits(me)
    out_first = [spread(sent.at[i], got.at[i], lambda p: p, mine, i) for i in range(2)]
    prepare(gates, weights, (1, 2))
    out_second = []
    for i in range(2):
        own, every = out_first[i]
        own.wait()
        every.wait_recv()
        later_layers(got.at[i], t, u, ready.at[i], weights)
        out_second.append(
            spread(ready.at[i], landed.at[i], lambda p: p % 2 * 64 + p // 2, me, 2 + i)
        )
    for _, every in out_first:
        every.wait_send()
    for own, every in out_second:
        own.wait()
        every.wait()


def finish(landed, out, stage, sems):
    def block(i, _):
        for r in range(8):
            v = [landed[j % 2, i * 16 + r * 2 + j // 2] for j in range(4)]
            for j, value in enumerate(trade_both(v)):
                stage[i, j // 2, r, j % 2] = value
        pltpu.make_async_copy(stage.at[i], out.at[i], sems.at[i]).start()
        return 0

    lax.fori_loop(0, 8, block, 0)

    def done(i, _):
        pltpu.make_async_copy(stage.at[i], out.at[i], sems.at[i]).wait()
        return 0

    lax.fori_loop(0, 8, done, 0)


def body(state, gates):
    rows = state.reshape(2, 4096, 128).transpose(1, 0, 2).reshape(8, 1024, 128)
    f32 = jnp.float32
    landed = pl.pallas_call(
        evolve,
        out_shape=jax.ShapeDtypeStruct((2, HALF, 128), f32),
        in_specs=[pl.BlockSpec(memory_space=pl.ANY), pl.BlockSpec(memory_space=pltpu.HBM)],
        out_specs=pl.BlockSpec(memory_space=pl.ANY),
        scratch_shapes=[
            pltpu.VMEM((8, 1024, 128), f32),
            pltpu.VMEM((8192, 128), f32),
            pltpu.VMEM((2, HALF, 128), f32),
            pltpu.VMEM((2, HALF, 128), f32),
            pltpu.VMEM((HALF, 128), f32),
            pltpu.VMEM((HALF, 128), f32),
            pltpu.VMEM((2, HALF, 128), f32),
            pltpu.VMEM((3, 2, 2, 64, 64), f32),
            pltpu.VMEM((6, 256, 256), jnp.bfloat16),
            pltpu.SemaphoreType.DMA((2,)),
            pltpu.SemaphoreType.DMA((4,)),
            pltpu.SemaphoreType.DMA((4,)),
            pltpu.SemaphoreType.DMA((4,)),
        ],
        compiler_params=pltpu.CompilerParams(
            collective_id=0, has_side_effects=True, vmem_limit_bytes=48 * 2**20
        ),
        name="evolve",
    )(rows, gates)
    shape = (8, 2, 8, 2, CHUNK, 128)
    out = pl.pallas_call(
        finish,
        out_shape=jax.ShapeDtypeStruct(shape, f32),
        in_specs=[pl.BlockSpec(memory_space=pltpu.VMEM)],
        out_specs=pl.BlockSpec(memory_space=pl.ANY),
        scratch_shapes=[pltpu.VMEM(shape, f32), pltpu.SemaphoreType.DMA((8,))],
        compiler_params=pltpu.CompilerParams(vmem_limit_bytes=16 * 2**20),
        name="finish",
    )(landed.reshape(2, 128, CHUNK, 128))
    return out.reshape(4096, 2, 128).transpose(1, 0, 2).reshape(2, -1)


def solution(mesh):
    placed = (P(None, ("qa", "qb")), P())
    return jax.shard_map(
        body, mesh=mesh, in_specs=placed, out_specs=P(None, ("qa", "qb")), check_vma=False
    )
```

```python
import functools

import jax
import jax.numpy as jnp
from jax import lax
from jax.experimental import pallas as pl
from jax.experimental.pallas import tpu as pltpu
from jax.sharding import PartitionSpec as P

MESH = pl.DeviceIdType.MESH
STEP = 13
FOUR = (0, 1, 2, 3)
ORDER = [1 + k * 116 % 127 for k in range(127)]
VMEM = 48 * 2**20
CHUNK = 32
HALF = 128 * CHUNK


def split(step):
    return step // 32, step // 8 % 4, step // 2 % 4, step % 2


def hops(step):
    return sum(min(d, 4 - d) for d in split(step)[:3])


class Torus:
    def __init__(self):
        qa, qb = lax.axis_index("qa"), lax.axis_index("qb")
        self.me = qa * 16 + qb
        x, z, core = lax.div(qa, 2), lax.div(qb, 4), lax.rem(qb, 2)
        y = lax.rem(lax.div(qb, 2), 2) * 2 + lax.rem(qa, 2)
        self.x = [lax.rem(x + d, 4) for d in range(4)]
        self.y = [lax.rem(y + d, 4) for d in range(4)]
        self.z = [lax.rem(z + d, 4) for d in range(4)]
        self.core = [core, 1 - core]
        self.y_low = [lax.rem(v, 2) for v in self.y]
        self.y_high = [lax.div(v, 2) for v in self.y]

    def partner(self, step):
        dx, dy, dz, dc = split(step)
        qa = self.x[dx] * 2 + self.y_low[dy]
        return qa, self.z[dz] * 4 + self.y_high[dy] * 2 + self.core[dc]


GREET = sorted(range(1, 128), key=lambda step: (-hops(step), step))


def reversed_bits(p):
    out = lax.rem(p, 2)
    for b in range(1, 7):
        out = out * 2 + lax.rem(lax.div(p, 1 << b), 2)
    return out


def trade(first, second, lane_bit):
    apart = 1 << lane_bit
    lane = lax.broadcasted_iota(jnp.int32, first.shape, first.ndim - 1)
    low = lane // apart % 2 == 0
    back = pltpu.roll(first, 128 - apart, first.ndim - 1)
    forth = pltpu.roll(second, apart, second.ndim - 1)
    return jnp.where(low, first, forth), jnp.where(low, back, second)


def trade_both(parts):
    lane = lax.broadcasted_iota(jnp.int32, parts[0].shape, parts[0].ndim - 1)
    odd, upper = lane // 32 % 2 == 1, lane // 64 == 1
    once = [jnp.where(odd, parts[(i + 1) % 4], parts[i]) for i in range(4)]
    skewed = [jnp.where(upper, once[(i + 2) % 4], once[i]) for i in range(4)]
    turned = skewed[:1] + [pltpu.roll(skewed[i], 32 * i, lane.ndim - 1) for i in range(1, 4)]
    once = [jnp.where(odd, turned[(i + 1) % 4], turned[i]) for i in range(4)]
    return [jnp.where(upper, once[(2 - j) % 4], once[-j % 4]) for j in range(4)]


def halves(x):
    high = x.astype(jnp.bfloat16)
    return high, (x - high.astype(jnp.float32)).astype(jnp.bfloat16)


def apply(weights, x):
    both = jnp.concatenate(halves(x), axis=0)
    out = jnp.dot(weights, both, preferred_element_type=jnp.float32)
    return out[:128] + out[128:]


def one_hot(wanted):
    column = lax.broadcasted_iota(jnp.int32, (128, 128), 1)
    return (column == wanted).astype(jnp.bfloat16)


def exactly(a, b, dims):
    return lax.dot_general(a, b, (dims, ((), ())), preferred_element_type=jnp.float32).astype(
        jnp.bfloat16
    )


def prepare(gates, weights, layers):
    row = lax.broadcasted_iota(jnp.int32, (128, 128), 0)
    low = row % 2 * 8 + row // 2 % 2 * 4 + row // 4 % 2 * 2 + row // 8 % 2
    turn = one_hot(row // 16 * 16 + low)
    natural = one_hot(row % 2 * 64 + row // 2 % 8 * 8 + row // 16)
    for layer in layers:
        for gate in range(2):
            real, imag = gates[layer, gate, 0], gates[layer, gate, 1]
            whole = jnp.concatenate(
                [
                    jnp.concatenate([real, -imag], axis=1),
                    jnp.concatenate([imag, real], axis=1),
                ],
                axis=0,
            )
            parts = halves(whole)
            if (layer, gate) == (0, 0):
                parts = [exactly(turn, part, ((1,), (0,))) for part in parts]
            if (layer, gate) == (0, 1):
                parts = [exactly(natural, part, ((1,), (0,))) for part in parts]
                parts = [exactly(part, natural, ((1,), (1,))) for part in parts]
            high, low_part = parts
            weights[2 * layer + gate, :128] = jnp.concatenate([high, high], axis=1)
            weights[2 * layer + gate, 128:] = jnp.concatenate([low_part, low_part], axis=1)


def second_gates(x, y, weights):
    def second_gate(i, _):
        m = i * 2
        parts = [x[h, pl.ds(m * 16, 32)] for h in range(8)]
        a = jnp.concatenate([p[:16] for p in parts], axis=0)
        b = jnp.concatenate([p[16:] for p in parts], axis=0)
        r = apply(weights[1], jnp.concatenate([a, b], axis=1))
        y[pl.ds(m, 128, stride=64)] = r[:, :128]
        y[pl.ds(m + 1, 128, stride=64)] = r[:, 128:]
        return 0

    lax.fori_loop(0, 32, second_gate, 0, unroll=8)


def first_gate(y, out, weights, q):
    a = y[pl.ds(q * 128, 128)]
    b = y[pl.ds(q * 128 + 4096, 128)]
    r = apply(weights[0], jnp.concatenate([a, b], axis=1))
    a = r[:, :128].reshape(4, 2, 16, 128)
    b = r[:, 128:].reshape(4, 2, 16, 128)
    for j, value in enumerate(trade_both([a[:, 0], a[:, 1], b[:, 0], b[:, 1]])):
        for s in range(2):
            for fifteen in range(2):
                to = ((q % 8) * 4 + q // 8) * 4 + fifteen * 2 + j // 2
                out[j % 2, pl.ds(to * CHUNK + s * 16, 16)] = value[s * 2 + fifteen]


def later_layers(x, t, u, out, weights):
    def put(ref, base, r):
        for s in range(2):
            ref[pl.ds(base + s * 2048, 64, stride=32)] = r[s * 64 : s * 64 + 64]

    def gate_10(i, _):
        cols = []
        for k in range(2):
            v = x[pl.ds((i * 2 + k) * 128, 128)].reshape(4, 2, 16, 128)
            cols.append(jnp.concatenate([v[:, s].reshape(64, 128) for s in range(2)], axis=0))
        r = apply(weights[2], jnp.concatenate(cols, axis=1))
        for k in range(2):
            put(t, i * 2 + k, r[:, k * 128 : k * 128 + 128])
        return 0

    lax.fori_loop(0, 16, gate_10, 0, unroll=8)

    def gate_11(i, _):
        cols = []
        for k in range(2):
            rows = []
            for s in range(2):
                v = t[pl.ds(s * 2048 + (i * 2 + k) * 64, 64)]
                rows.extend(trade(v[:32], v[32:], 5))
            cols.append(jnp.concatenate(rows, axis=0))
        r = apply(weights[3], jnp.concatenate(cols, axis=1))
        for k in range(2):
            put(u, i * 2 + k, r[:, k * 128 : k * 128 + 128])
        return 0

    lax.fori_loop(0, 16, gate_11, 0, unroll=8)

    def gate_20(i, _):
        cols = []
        for k in range(2):
            rows = [u[pl.ds(s * 2048 + (i * 2 + k) * 64, 64)] for s in range(2)]
            cols.append(jnp.concatenate(rows, axis=0))
        r = apply(weights[4], jnp.concatenate(cols, axis=1))
        for k in range(2):
            put(t, i * 2 + k, r[:, k * 128 : k * 128 + 128])
        return 0

    lax.fori_loop(0, 16, gate_20, 0, unroll=8)

    def gate_21(i, _):
        cols = []
        for k in range(2):
            rows = []
            base = (i // 8 * 32 + i % 8 * 2 + k) * 32
            for s in range(2):
                v0 = t[pl.ds(s * 2048 + base, 32)]
                v1 = t[pl.ds(s * 2048 + base + 512, 32)]
                c = trade_both([v0[:16], v1[:16], v0[16:], v1[16:]])
                rows.extend([c[0], c[2], c[1], c[3]])
            cols.append(jnp.concatenate(rows, axis=0))
        r = apply(weights[5], jnp.concatenate(cols, axis=1))
        for k in range(2):
            for s in range(2):
                base = i // 8 * 2048 + (i % 8 * 2 + k) * 2 + s
                out[pl.ds(base, 64, stride=32)] = r[s * 64 : s * 64 + 64, k * 128 : k * 128 + 128]
        return 0

    lax.fori_loop(0, 16, gate_21, 0, unroll=8)


def evolve(
    x_hbm, gates_hbm, landed, x, y, sent, got, t, u, ready, gates, weights,
    load_sems, own_sems, send_sems, recv_sems,
):
    load_gates = pltpu.make_async_copy(gates_hbm, gates, load_sems.at[0])
    load_gates.start()
    load = pltpu.make_async_copy(x_hbm, x, load_sems.at[1])
    load.start()
    barrier = pltpu.get_barrier_semaphore()
    torus = Torus()
    me = torus.me
    for step in GREET:
        pl.semaphore_signal(barrier, inc=1, device_id=torus.partner(step), device_id_type=MESH)

    def remote(step, source, target, chunk_of, slot, number):
        qa, qb = torus.partner(step)
        return pltpu.make_async_remote_copy(
            src_ref=source.at[pl.ds(chunk_of(qa * 16 + qb) * CHUNK, CHUNK)],
            dst_ref=target.at[pl.ds(slot * CHUNK, CHUNK)],
            send_sem=send_sems.at[number],
            recv_sem=recv_sems.at[number],
            device_id=(qa, qb),
            device_id_type=MESH,
        )

    def keep(source, target, chunk_of, slot, number):
        return pltpu.make_async_copy(
            source.at[pl.ds(chunk_of(me) * CHUNK, CHUNK)],
            target.at[pl.ds(slot * CHUNK, CHUNK)],
            own_sems.at[number],
        )

    def every(source, target, number):
        return pltpu.make_async_remote_copy(
            src_ref=source.at[pl.ds(0, 127 * CHUNK)],
            dst_ref=target.at[pl.ds(0, 127 * CHUNK)],
            send_sem=send_sems.at[number],
            recv_sem=recv_sems.at[number],
            device_id=torus.partner(1),
            device_id_type=MESH,
        )

    def straight(p):
        return p

    def twisted(p):
        return lax.rem(p, 2) * 64 + lax.div(p, 2)

    mine = reversed_bits(me)
    load_gates.wait()
    prepare(gates, weights, (0,))
    load.wait()
    second_gates(x, y, weights)
    for block in range(4):
        steps = [(block * 8 + i + 1) * STEP % 32 for i in range(8)]
        for step in steps:
            q = torus.z[step // 2 % 4] * 8 + torus.x[step // 8] * 2 + torus.y_low[step % 2]
            first_gate(y, sent, weights, q)
        if block == 0:
            pl.semaphore_wait(barrier, 127)
        for e in FOUR:
            for step in steps:
                k = step // 8 * 32 + (step % 2 + e // 2 * 2) * 8 + step // 2 % 4 * 2 + e % 2
                if k:
                    remote(k, sent.at[0], got.at[0], straight, mine, 0).start()
    keep(sent.at[0], got.at[0], straight, mine, 0).start()
    for step in ORDER:
        remote(step, sent.at[1], got.at[1], straight, mine, 1).start()
    keep(sent.at[1], got.at[1], straight, mine, 1).start()
    prepare(gates, weights, (1, 2))

    def middle(i, _):
        keep(sent.at[i], got.at[i], straight, mine, i).wait()
        every(sent.at[i], got.at[i], i).wait_recv()
        later_layers(got.at[i], t, u, ready.at[i], weights)
        for step in ORDER:
            remote(step, ready.at[i], landed.at[i], twisted, me, 2 + i).start()
        keep(ready.at[i], landed.at[i], twisted, me, 2 + i).start()
        return 0

    lax.fori_loop(0, 2, middle, 0)
    for i in range(2):
        every(sent.at[i], got.at[i], i).wait_send()
        keep(ready.at[i], landed.at[i], twisted, me, 2 + i).wait()
        every(ready.at[i], landed.at[i], 2 + i).wait()


def finish(landed, out, stage, sems):
    def block(i, _):
        for r in range(8):
            v = [landed[j % 2, i * 16 + r * 2 + j // 2] for j in range(4)]
            for j, value in enumerate(trade_both(v)):
                stage[i, j // 2, r, j % 2] = value
        pltpu.make_async_copy(stage.at[i], out.at[i], sems.at[i]).start()
        return 0

    lax.fori_loop(0, 8, block, 0)

    def done(i, _):
        pltpu.make_async_copy(stage.at[i], out.at[i], sems.at[i]).wait()
        return 0

    lax.fori_loop(0, 8, done, 0)


def body(state, gates):
    rows = state.reshape(2, 4096, 128).transpose(1, 0, 2).reshape(8, 1024, 128)
    f32 = jnp.float32
    landed = pl.pallas_call(
        evolve,
        out_shape=jax.ShapeDtypeStruct((2, HALF, 128), f32),
        in_specs=[pl.BlockSpec(memory_space=pl.ANY), pl.BlockSpec(memory_space=pltpu.HBM)],
        out_specs=pl.BlockSpec(memory_space=pl.ANY),
        scratch_shapes=[
            pltpu.VMEM((8, 1024, 128), f32),
            pltpu.VMEM((8192, 128), f32),
            pltpu.VMEM((2, HALF, 128), f32),
            pltpu.VMEM((2, HALF, 128), f32),
            pltpu.VMEM((HALF, 128), f32),
            pltpu.VMEM((HALF, 128), f32),
            pltpu.VMEM((2, HALF, 128), f32),
            pltpu.VMEM((3, 2, 2, 64, 64), f32),
            pltpu.VMEM((6, 256, 256), jnp.bfloat16),
            pltpu.SemaphoreType.DMA((2,)),
            pltpu.SemaphoreType.DMA((4,)),
            pltpu.SemaphoreType.DMA((4,)),
            pltpu.SemaphoreType.DMA((4,)),
        ],
        compiler_params=pltpu.CompilerParams(
            collective_id=0, has_side_effects=True, vmem_limit_bytes=VMEM
        ),
        name="evolve",
    )(rows, gates)
    shape = (8, 2, 8, 2, CHUNK, 128)
    out = pl.pallas_call(
        finish,
        out_shape=jax.ShapeDtypeStruct(shape, f32),
        in_specs=[pl.BlockSpec(memory_space=pltpu.VMEM)],
        out_specs=pl.BlockSpec(memory_space=pl.ANY),
        scratch_shapes=[pltpu.VMEM(shape, f32), pltpu.SemaphoreType.DMA((8,))],
        compiler_params=pltpu.CompilerParams(vmem_limit_bytes=16 * 2**20),
        name="finish",
    )(landed.reshape(2, 128, CHUNK, 128))
    return out.reshape(4096, 2, 128).transpose(1, 0, 2).reshape(2, -1)


def solution(mesh):
    placed = (P(None, ("qa", "qb")), P())
    return jax.shard_map(
        body, mesh=mesh, in_specs=placed, out_specs=P(None, ("qa", "qb")), check_vma=False
    )
```

```python
import functools

import jax
import jax.numpy as jnp
from jax import lax
from jax.experimental import pallas as pl
from jax.experimental.pallas import tpu as pltpu
from jax.sharding import PartitionSpec as P

MESH = pl.DeviceIdType.MESH
STEP = 13
FOUR = (0, 1, 2, 3)
BLOCKS = (4, 4, 8, 8, 8)
ORDER = [1 + k * 41 % 127 for k in range(127)]
VMEM = 48 * 2**20
CHUNK = 32
HALF = 128 * CHUNK


def split(step):
    return step // 32, step // 8 % 4, step // 2 % 4, step % 2


def hops(step):
    return sum(min(d, 4 - d) for d in split(step)[:3])


class Torus:
    def __init__(self):
        qa, qb = lax.axis_index("qa"), lax.axis_index("qb")
        self.me = qa * 16 + qb
        x, z, core = lax.div(qa, 2), lax.div(qb, 4), lax.rem(qb, 2)
        y = lax.rem(lax.div(qb, 2), 2) * 2 + lax.rem(qa, 2)
        self.x = [lax.rem(x + d, 4) for d in range(4)]
        self.y = [lax.rem(y + d, 4) for d in range(4)]
        self.z = [lax.rem(z + d, 4) for d in range(4)]
        self.core = [core, 1 - core]
        self.y_low = [lax.rem(v, 2) for v in self.y]
        self.y_high = [lax.div(v, 2) for v in self.y]

    def partner(self, step):
        dx, dy, dz, dc = split(step)
        qa = self.x[dx] * 2 + self.y_low[dy]
        return qa, self.z[dz] * 4 + self.y_high[dy] * 2 + self.core[dc]


GREET = sorted(range(1, 128), key=lambda step: (-hops(step), step))


def reversed_bits(p):
    out = lax.rem(p, 2)
    for b in range(1, 7):
        out = out * 2 + lax.rem(lax.div(p, 1 << b), 2)
    return out


def trade(first, second, lane_bit):
    apart = 1 << lane_bit
    lane = lax.broadcasted_iota(jnp.int32, first.shape, first.ndim - 1)
    low = lane // apart % 2 == 0
    back = pltpu.roll(first, 128 - apart, first.ndim - 1)
    forth = pltpu.roll(second, apart, second.ndim - 1)
    return jnp.where(low, first, forth), jnp.where(low, back, second)


def trade_both(parts):
    lane = lax.broadcasted_iota(jnp.int32, parts[0].shape, parts[0].ndim - 1)
    odd, upper = lane // 32 % 2 == 1, lane // 64 == 1
    once = [jnp.where(odd, parts[(i + 1) % 4], parts[i]) for i in range(4)]
    skewed = [jnp.where(upper, once[(i + 2) % 4], once[i]) for i in range(4)]
    turned = skewed[:1] + [pltpu.roll(skewed[i], 32 * i, lane.ndim - 1) for i in range(1, 4)]
    once = [jnp.where(odd, turned[(i + 1) % 4], turned[i]) for i in range(4)]
    return [jnp.where(upper, once[(2 - j) % 4], once[-j % 4]) for j in range(4)]


def halves(x):
    high = x.astype(jnp.bfloat16)
    return high, (x - high.astype(jnp.float32)).astype(jnp.bfloat16)


def apply(weights, x):
    both = jnp.concatenate(halves(x), axis=0)
    out = jnp.dot(weights, both, preferred_element_type=jnp.float32)
    return out[:128] + out[128:]


def one_hot(wanted):
    column = lax.broadcasted_iota(jnp.int32, (128, 128), 1)
    return (column == wanted).astype(jnp.bfloat16)


def exactly(a, b, dims):
    return lax.dot_general(a, b, (dims, ((), ())), preferred_element_type=jnp.float32).astype(
        jnp.bfloat16
    )


def prepare(gates, weights, layers):
    row = lax.broadcasted_iota(jnp.int32, (128, 128), 0)
    low = row % 2 * 8 + row // 2 % 2 * 4 + row // 4 % 2 * 2 + row // 8 % 2
    turn = one_hot(row // 16 * 16 + low)
    natural = one_hot(row % 2 * 64 + row // 2 % 8 * 8 + row // 16)
    for layer in layers:
        for gate in range(2):
            real, imag = gates[layer, gate, 0], gates[layer, gate, 1]
            whole = jnp.concatenate(
                [
                    jnp.concatenate([real, -imag], axis=1),
                    jnp.concatenate([imag, real], axis=1),
                ],
                axis=0,
            )
            parts = halves(whole)
            if (layer, gate) == (0, 0):
                parts = [exactly(turn, part, ((1,), (0,))) for part in parts]
            if (layer, gate) == (0, 1):
                parts = [exactly(natural, part, ((1,), (0,))) for part in parts]
                parts = [exactly(part, natural, ((1,), (1,))) for part in parts]
            high, low_part = parts
            weights[2 * layer + gate, :128] = jnp.concatenate([high, high], axis=1)
            weights[2 * layer + gate, 128:] = jnp.concatenate([low_part, low_part], axis=1)


def second_gates(x, y, weights):
    def second_gate(i, _):
        m = i * 2
        parts = [x[h, pl.ds(m * 16, 32)] for h in range(8)]
        a = jnp.concatenate([p[:16] for p in parts], axis=0)
        b = jnp.concatenate([p[16:] for p in parts], axis=0)
        r = apply(weights[1], jnp.concatenate([a, b], axis=1))
        y[pl.ds(m, 128, stride=64)] = r[:, :128]
        y[pl.ds(m + 1, 128, stride=64)] = r[:, 128:]
        return 0

    lax.fori_loop(0, 32, second_gate, 0, unroll=8)


def first_gate(y, out, weights, q):
    a = y[pl.ds(q * 128, 128)]
    b = y[pl.ds(q * 128 + 4096, 128)]
    r = apply(weights[0], jnp.concatenate([a, b], axis=1))
    a = r[:, :128].reshape(4, 2, 16, 128)
    b = r[:, 128:].reshape(4, 2, 16, 128)
    for j, value in enumerate(trade_both([a[:, 0], a[:, 1], b[:, 0], b[:, 1]])):
        for s in range(2):
            for fifteen in range(2):
                to = ((q % 8) * 4 + q // 8) * 4 + fifteen * 2 + j // 2
                out[j % 2, pl.ds(to * CHUNK + s * 16, 16)] = value[s * 2 + fifteen]


def later_layers(x, t, u, out, weights):
    def put(ref, base, r):
        for s in range(2):
            ref[pl.ds(base + s * 2048, 64, stride=32)] = r[s * 64 : s * 64 + 64]

    def gate_10(i, _):
        cols = []
        for k in range(2):
            v = x[pl.ds((i * 2 + k) * 128, 128)].reshape(4, 2, 16, 128)
            cols.append(jnp.concatenate([v[:, s].reshape(64, 128) for s in range(2)], axis=0))
        r = apply(weights[2], jnp.concatenate(cols, axis=1))
        for k in range(2):
            put(t, i * 2 + k, r[:, k * 128 : k * 128 + 128])
        return 0

    lax.fori_loop(0, 16, gate_10, 0, unroll=8)

    def gate_11(i, _):
        cols = []
        for k in range(2):
            rows = []
            for s in range(2):
                v = t[pl.ds(s * 2048 + (i * 2 + k) * 64, 64)]
                rows.extend(trade(v[:32], v[32:], 5))
            cols.append(jnp.concatenate(rows, axis=0))
        r = apply(weights[3], jnp.concatenate(cols, axis=1))
        for k in range(2):
            put(u, i * 2 + k, r[:, k * 128 : k * 128 + 128])
        return 0

    lax.fori_loop(0, 16, gate_11, 0, unroll=8)

    def gate_20(i, _):
        cols = []
        for k in range(2):
            rows = [u[pl.ds(s * 2048 + (i * 2 + k) * 64, 64)] for s in range(2)]
            cols.append(jnp.concatenate(rows, axis=0))
        r = apply(weights[4], jnp.concatenate(cols, axis=1))
        for k in range(2):
            put(t, i * 2 + k, r[:, k * 128 : k * 128 + 128])
        return 0

    lax.fori_loop(0, 16, gate_20, 0, unroll=8)

    def gate_21(i, _):
        cols = []
        for k in range(2):
            rows = []
            base = (i // 8 * 32 + i % 8 * 2 + k) * 32
            for s in range(2):
                v0 = t[pl.ds(s * 2048 + base, 32)]
                v1 = t[pl.ds(s * 2048 + base + 512, 32)]
                c = trade_both([v0[:16], v1[:16], v0[16:], v1[16:]])
                rows.extend([c[0], c[2], c[1], c[3]])
            cols.append(jnp.concatenate(rows, axis=0))
        r = apply(weights[5], jnp.concatenate(cols, axis=1))
        for k in range(2):
            for s in range(2):
                base = i // 8 * 2048 + (i % 8 * 2 + k) * 2 + s
                out[pl.ds(base, 64, stride=32)] = r[s * 64 : s * 64 + 64, k * 128 : k * 128 + 128]
        return 0

    lax.fori_loop(0, 16, gate_21, 0, unroll=8)


def evolve(
    x_hbm, gates_hbm, landed, x, y, sent, got, t, u, ready, gates, weights,
    load_sems, own_sems, send_sems, recv_sems,
):
    load_gates = pltpu.make_async_copy(gates_hbm, gates, load_sems.at[0])
    load_gates.start()
    load = pltpu.make_async_copy(x_hbm, x, load_sems.at[1])
    load.start()
    barrier = pltpu.get_barrier_semaphore()
    torus = Torus()
    me = torus.me
    for step in GREET:
        pl.semaphore_signal(barrier, inc=1, device_id=torus.partner(step), device_id_type=MESH)

    def remote(step, source, target, chunk_of, slot, number):
        qa, qb = torus.partner(step)
        return pltpu.make_async_remote_copy(
            src_ref=source.at[pl.ds(chunk_of(qa * 16 + qb) * CHUNK, CHUNK)],
            dst_ref=target.at[pl.ds(slot * CHUNK, CHUNK)],
            send_sem=send_sems.at[number],
            recv_sem=recv_sems.at[number],
            device_id=(qa, qb),
            device_id_type=MESH,
        )

    def keep(source, target, chunk_of, slot, number):
        return pltpu.make_async_copy(
            source.at[pl.ds(chunk_of(me) * CHUNK, CHUNK)],
            target.at[pl.ds(slot * CHUNK, CHUNK)],
            own_sems.at[number],
        )

    def every(source, target, number):
        return pltpu.make_async_remote_copy(
            src_ref=source.at[pl.ds(0, 127 * CHUNK)],
            dst_ref=target.at[pl.ds(0, 127 * CHUNK)],
            send_sem=send_sems.at[number],
            recv_sem=recv_sems.at[number],
            device_id=torus.partner(1),
            device_id_type=MESH,
        )

    def straight(p):
        return p

    def twisted(p):
        return lax.rem(p, 2) * 64 + lax.div(p, 2)

    mine = reversed_bits(me)
    load_gates.wait()
    prepare(gates, weights, (0,))
    load.wait()
    second_gates(x, y, weights)
    done = 0
    for size in BLOCKS:
        steps = [(done + i + 1) * STEP % 32 for i in range(size)]
        for step in steps:
            q = torus.z[step // 2 % 4] * 8 + torus.x[step // 8] * 2 + torus.y_low[step % 2]
            first_gate(y, sent, weights, q)
        if done == 0:
            pl.semaphore_wait(barrier, 127)
        for e in FOUR:
            for step in steps:
                k = step // 8 * 32 + (step % 2 + e // 2 * 2) * 8 + step // 2 % 4 * 2 + e % 2
                if k:
                    remote(k, sent.at[0], got.at[0], straight, mine, 0).start()
        done += size
    keep(sent.at[0], got.at[0], straight, mine, 0).start()
    for step in ORDER:
        remote(step, sent.at[1], got.at[1], straight, mine, 1).start()
    keep(sent.at[1], got.at[1], straight, mine, 1).start()
    prepare(gates, weights, (1, 2))

    def middle(i, _):
        keep(sent.at[i], got.at[i], straight, mine, i).wait()
        every(sent.at[i], got.at[i], i).wait_recv()
        later_layers(got.at[i], t, u, ready.at[i], weights)
        for step in ORDER:
            remote(step, ready.at[i], landed.at[i], twisted, me, 2 + i).start()
        keep(ready.at[i], landed.at[i], twisted, me, 2 + i).start()
        return 0

    lax.fori_loop(0, 2, middle, 0)
    for i in range(2):
        every(sent.at[i], got.at[i], i).wait_send()
        keep(ready.at[i], landed.at[i], twisted, me, 2 + i).wait()
        every(ready.at[i], landed.at[i], 2 + i).wait()


def finish(landed, out, stage, sems):
    def block(i, _):
        for r in range(8):
            v = [landed[j % 2, i * 16 + r * 2 + j // 2] for j in range(4)]
            for j, value in enumerate(trade_both(v)):
                stage[i, j // 2, r, j % 2] = value
        pltpu.make_async_copy(stage.at[i], out.at[i], sems.at[i]).start()
        return 0

    lax.fori_loop(0, 8, block, 0)

    def done(i, _):
        pltpu.make_async_copy(stage.at[i], out.at[i], sems.at[i]).wait()
        return 0

    lax.fori_loop(0, 8, done, 0)


def body(state, gates):
    rows = state.reshape(2, 4096, 128).transpose(1, 0, 2).reshape(8, 1024, 128)
    f32 = jnp.float32
    landed = pl.pallas_call(
        evolve,
        out_shape=jax.ShapeDtypeStruct((2, HALF, 128), f32),
        in_specs=[pl.BlockSpec(memory_space=pl.ANY), pl.BlockSpec(memory_space=pltpu.HBM)],
        out_specs=pl.BlockSpec(memory_space=pl.ANY),
        scratch_shapes=[
            pltpu.VMEM((8, 1024, 128), f32),
            pltpu.VMEM((8192, 128), f32),
            pltpu.VMEM((2, HALF, 128), f32),
            pltpu.VMEM((2, HALF, 128), f32),
            pltpu.VMEM((HALF, 128), f32),
            pltpu.VMEM((HALF, 128), f32),
            pltpu.VMEM((2, HALF, 128), f32),
            pltpu.VMEM((3, 2, 2, 64, 64), f32),
            pltpu.VMEM((6, 256, 256), jnp.bfloat16),
            pltpu.SemaphoreType.DMA((2,)),
            pltpu.SemaphoreType.DMA((4,)),
            pltpu.SemaphoreType.DMA((4,)),
            pltpu.SemaphoreType.DMA((4,)),
        ],
        compiler_params=pltpu.CompilerParams(
            collective_id=0, has_side_effects=True, vmem_limit_bytes=VMEM
        ),
        name="evolve",
    )(rows, pltpu.with_memory_space_constraint(gates, pltpu.HBM))
    shape = (8, 2, 8, 2, CHUNK, 128)
    out = pl.pallas_call(
        finish,
        out_shape=jax.ShapeDtypeStruct(shape, f32),
        in_specs=[pl.BlockSpec(memory_space=pltpu.VMEM)],
        out_specs=pl.BlockSpec(memory_space=pl.ANY),
        scratch_shapes=[pltpu.VMEM(shape, f32), pltpu.SemaphoreType.DMA((8,))],
        compiler_params=pltpu.CompilerParams(vmem_limit_bytes=16 * 2**20),
        name="finish",
    )(landed.reshape(2, 128, CHUNK, 128))
    return out.reshape(4096, 2, 128).transpose(1, 0, 2).reshape(2, -1)


def solution(mesh):
    placed = (P(None, ("qa", "qb")), P())
    return jax.shard_map(
        body, mesh=mesh, in_specs=placed, out_specs=P(None, ("qa", "qb")), check_vma=False
    )
```

```python
import functools

import jax
import jax.numpy as jnp
from jax import lax
from jax.experimental import pallas as pl
from jax.experimental.pallas import tpu as pltpu
from jax.sharding import PartitionSpec as P

MESH = pl.DeviceIdType.MESH
STEP = 13
FOUR = (0, 1, 2, 3)
BLOCKS = (4, 4, 8, 8, 8)
ORDER = [1 + k * 41 % 127 for k in range(127)]
VMEM = 48 * 2**20
CHUNK = 32
HALF = 128 * CHUNK


def split(step):
    return step // 32, step // 8 % 4, step // 2 % 4, step % 2


def hops(step):
    return sum(min(d, 4 - d) for d in split(step)[:3])


class Torus:
    def __init__(self):
        qa, qb = lax.axis_index("qa"), lax.axis_index("qb")
        self.me = qa * 16 + qb
        x, z, core = lax.div(qa, 2), lax.div(qb, 4), lax.rem(qb, 2)
        y = lax.rem(lax.div(qb, 2), 2) * 2 + lax.rem(qa, 2)
        self.x = [lax.rem(x + d, 4) for d in range(4)]
        self.y = [lax.rem(y + d, 4) for d in range(4)]
        self.z = [lax.rem(z + d, 4) for d in range(4)]
        self.core = [core, 1 - core]
        self.y_low = [lax.rem(v, 2) for v in self.y]
        self.y_high = [lax.div(v, 2) for v in self.y]

    def partner(self, step):
        dx, dy, dz, dc = split(step)
        qa = self.x[dx] * 2 + self.y_low[dy]
        return qa, self.z[dz] * 4 + self.y_high[dy] * 2 + self.core[dc]


GREET = sorted(range(1, 128), key=lambda step: (-hops(step), step))


def reversed_bits(p):
    out = lax.rem(p, 2)
    for b in range(1, 7):
        out = out * 2 + lax.rem(lax.div(p, 1 << b), 2)
    return out


def trade(first, second, lane_bit):
    apart = 1 << lane_bit
    lane = lax.broadcasted_iota(jnp.int32, first.shape, first.ndim - 1)
    low = lane // apart % 2 == 0
    back = pltpu.roll(first, 128 - apart, first.ndim - 1)
    forth = pltpu.roll(second, apart, second.ndim - 1)
    return jnp.where(low, first, forth), jnp.where(low, back, second)


def trade_both(parts):
    lane = lax.broadcasted_iota(jnp.int32, parts[0].shape, parts[0].ndim - 1)
    odd, upper = lane // 32 % 2 == 1, lane // 64 == 1
    once = [jnp.where(odd, parts[(i + 1) % 4], parts[i]) for i in range(4)]
    skewed = [jnp.where(upper, once[(i + 2) % 4], once[i]) for i in range(4)]
    turned = skewed[:1] + [pltpu.roll(skewed[i], 32 * i, lane.ndim - 1) for i in range(1, 4)]
    once = [jnp.where(odd, turned[(i + 1) % 4], turned[i]) for i in range(4)]
    return [jnp.where(upper, once[(2 - j) % 4], once[-j % 4]) for j in range(4)]


def halves(x):
    high = x.astype(jnp.bfloat16)
    return high, (x - high.astype(jnp.float32)).astype(jnp.bfloat16)


def apply(weights, x):
    both = jnp.concatenate(halves(x), axis=0)
    out = jnp.dot(weights, both, preferred_element_type=jnp.float32)
    return out[:128] + out[128:]


def one_hot(wanted):
    column = lax.broadcasted_iota(jnp.int32, (128, 128), 1)
    return (column == wanted).astype(jnp.bfloat16)


def exactly(a, b, dims):
    return lax.dot_general(a, b, (dims, ((), ())), preferred_element_type=jnp.float32).astype(
        jnp.bfloat16
    )


def prepare(gates, weights, layers):
    row = lax.broadcasted_iota(jnp.int32, (128, 128), 0)
    low = row % 2 * 8 + row // 2 % 2 * 4 + row // 4 % 2 * 2 + row // 8 % 2
    turn = one_hot(row // 16 * 16 + low)
    natural = one_hot(row % 2 * 64 + row // 2 % 8 * 8 + row // 16)
    for layer in layers:
        for gate in range(2):
            real, imag = gates[layer, gate, 0], gates[layer, gate, 1]
            whole = jnp.concatenate(
                [
                    jnp.concatenate([real, -imag], axis=1),
                    jnp.concatenate([imag, real], axis=1),
                ],
                axis=0,
            )
            parts = halves(whole)
            if (layer, gate) == (0, 0):
                parts = [exactly(turn, part, ((1,), (0,))) for part in parts]
            if (layer, gate) == (0, 1):
                parts = [exactly(natural, part, ((1,), (0,))) for part in parts]
                parts = [exactly(part, natural, ((1,), (1,))) for part in parts]
            high, low_part = parts
            weights[2 * layer + gate, :128] = jnp.concatenate([high, high], axis=1)
            weights[2 * layer + gate, 128:] = jnp.concatenate([low_part, low_part], axis=1)


def second_gates(x, y, weights):
    def second_gate(i, _):
        m = i * 2
        parts = [x[h, pl.ds(m * 16, 32)] for h in range(8)]
        a = jnp.concatenate([p[:16] for p in parts], axis=0)
        b = jnp.concatenate([p[16:] for p in parts], axis=0)
        r = apply(weights[1], jnp.concatenate([a, b], axis=1))
        y[pl.ds(m, 128, stride=64)] = r[:, :128]
        y[pl.ds(m + 1, 128, stride=64)] = r[:, 128:]
        return 0

    lax.fori_loop(0, 32, second_gate, 0, unroll=8)


def first_gate(y, out, weights, q):
    a = y[pl.ds(q * 128, 128)]
    b = y[pl.ds(q * 128 + 4096, 128)]
    r = apply(weights[0], jnp.concatenate([a, b], axis=1))
    a = r[:, :128].reshape(4, 2, 16, 128)
    b = r[:, 128:].reshape(4, 2, 16, 128)
    for j, value in enumerate(trade_both([a[:, 0], a[:, 1], b[:, 0], b[:, 1]])):
        for s in range(2):
            for fifteen in range(2):
                to = ((q % 8) * 4 + q // 8) * 4 + fifteen * 2 + j // 2
                out[j % 2, pl.ds(to * CHUNK + s * 16, 16)] = value[s * 2 + fifteen]


def later_layers(x, t, u, out, weights):
    def put(ref, base, r):
        for s in range(2):
            ref[pl.ds(base + s * 2048, 64, stride=32)] = r[s * 64 : s * 64 + 64]

    def gate_10(i, _):
        cols = []
        for k in range(2):
            v = x[pl.ds((i * 2 + k) * 128, 128)].reshape(4, 2, 16, 128)
            cols.append(jnp.concatenate([v[:, s].reshape(64, 128) for s in range(2)], axis=0))
        r = apply(weights[2], jnp.concatenate(cols, axis=1))
        for k in range(2):
            put(t, i * 2 + k, r[:, k * 128 : k * 128 + 128])
        return 0

    lax.fori_loop(0, 16, gate_10, 0, unroll=8)

    def gate_11(i, _):
        cols = []
        for k in range(2):
            rows = []
            for s in range(2):
                v = t[pl.ds(s * 2048 + (i * 2 + k) * 64, 64)]
                rows.extend(trade(v[:32], v[32:], 5))
            cols.append(jnp.concatenate(rows, axis=0))
        r = apply(weights[3], jnp.concatenate(cols, axis=1))
        for k in range(2):
            put(u, i * 2 + k, r[:, k * 128 : k * 128 + 128])
        return 0

    lax.fori_loop(0, 16, gate_11, 0, unroll=8)

    def gate_20(i, _):
        cols = []
        for k in range(2):
            rows = [u[pl.ds(s * 2048 + (i * 2 + k) * 64, 64)] for s in range(2)]
            cols.append(jnp.concatenate(rows, axis=0))
        r = apply(weights[4], jnp.concatenate(cols, axis=1))
        for k in range(2):
            put(t, i * 2 + k, r[:, k * 128 : k * 128 + 128])
        return 0

    lax.fori_loop(0, 16, gate_20, 0, unroll=8)

    def gate_21(i, _):
        cols = []
        for k in range(2):
            rows = []
            base = (i // 8 * 32 + i % 8 * 2 + k) * 32
            for s in range(2):
                v0 = t[pl.ds(s * 2048 + base, 32)]
                v1 = t[pl.ds(s * 2048 + base + 512, 32)]
                c = trade_both([v0[:16], v1[:16], v0[16:], v1[16:]])
                rows.extend([c[0], c[2], c[1], c[3]])
            cols.append(jnp.concatenate(rows, axis=0))
        r = apply(weights[5], jnp.concatenate(cols, axis=1))
        for k in range(2):
            for s in range(2):
                base = i // 8 * 2048 + (i % 8 * 2 + k) * 2 + s
                out[pl.ds(base, 64, stride=32)] = r[s * 64 : s * 64 + 64, k * 128 : k * 128 + 128]
        return 0

    lax.fori_loop(0, 16, gate_21, 0, unroll=8)


def evolve(
    x_hbm, gates_hbm, landed, x, y, sent, got, t, u, ready, gates, weights,
    load_sems, own_sems, send_sems, recv_sems,
):
    load_gates = pltpu.make_async_copy(gates_hbm, gates, load_sems.at[0])
    load_gates.start()
    load = pltpu.make_async_copy(x_hbm, x, load_sems.at[1])
    load.start()
    barrier = pltpu.get_barrier_semaphore()
    torus = Torus()
    me = torus.me
    for step in GREET:
        pl.semaphore_signal(barrier, inc=1, device_id=torus.partner(step), device_id_type=MESH)

    def remote(step, source, target, chunk_of, slot, number):
        qa, qb = torus.partner(step)
        return pltpu.make_async_remote_copy(
            src_ref=source.at[pl.ds(chunk_of(qa * 16 + qb) * CHUNK, CHUNK)],
            dst_ref=target.at[pl.ds(slot * CHUNK, CHUNK)],
            send_sem=send_sems.at[number],
            recv_sem=recv_sems.at[number],
            device_id=(qa, qb),
            device_id_type=MESH,
        )

    def keep(source, target, chunk_of, slot, number):
        return pltpu.make_async_copy(
            source.at[pl.ds(chunk_of(me) * CHUNK, CHUNK)],
            target.at[pl.ds(slot * CHUNK, CHUNK)],
            own_sems.at[number],
        )

    def every(source, target, number):
        return pltpu.make_async_remote_copy(
            src_ref=source.at[pl.ds(0, 127 * CHUNK)],
            dst_ref=target.at[pl.ds(0, 127 * CHUNK)],
            send_sem=send_sems.at[number],
            recv_sem=recv_sems.at[number],
            device_id=torus.partner(1),
            device_id_type=MESH,
        )

    def straight(p):
        return p

    def twisted(p):
        return lax.rem(p, 2) * 64 + lax.div(p, 2)

    mine = reversed_bits(me)
    load_gates.wait()
    prepare(gates, weights, (0,))
    load.wait()
    second_gates(x, y, weights)
    done = 0
    for size in BLOCKS:
        steps = [(done + i + 1) * STEP % 32 for i in range(size)]
        for step in steps:
            q = torus.z[step // 2 % 4] * 8 + torus.x[step // 8] * 2 + torus.y_low[step % 2]
            first_gate(y, sent, weights, q)
        if done == 0:
            pl.semaphore_wait(barrier, 127)
        for e in FOUR:
            for step in steps:
                k = step // 8 * 32 + (step % 2 + e // 2 * 2) * 8 + step // 2 % 4 * 2 + e % 2
                if k:
                    remote(k, sent.at[0], got.at[0], straight, mine, 0).start()
        done += size
    keep(sent.at[0], got.at[0], straight, mine, 0).start()
    for step in ORDER:
        remote(step, sent.at[1], got.at[1], straight, mine, 1).start()
    keep(sent.at[1], got.at[1], straight, mine, 1).start()
    prepare(gates, weights, (1, 2))

    def middle(i, _):
        keep(sent.at[i], got.at[i], straight, mine, i).wait()
        every(sent.at[i], got.at[i], i).wait_recv()
        later_layers(got.at[i], t, u, ready.at[i], weights)
        for step in ORDER:
            remote(step, ready.at[i], landed.at[i], twisted, me, 2 + i).start()
        keep(ready.at[i], landed.at[i], twisted, me, 2 + i).start()
        return 0

    lax.fori_loop(0, 2, middle, 0)
    for i in range(2):
        every(sent.at[i], got.at[i], i).wait_send()
        keep(ready.at[i], landed.at[i], twisted, me, 2 + i).wait()
        every(ready.at[i], landed.at[i], 2 + i).wait()


def finish(landed, out, stage, sems):
    def block(i, _):
        for r in range(8):
            v = [landed[j % 2, i * 16 + r * 2 + j // 2] for j in range(4)]
            for j, value in enumerate(trade_both(v)):
                stage[i, j // 2, r, j % 2] = value
        pltpu.make_async_copy(stage.at[i], out.at[i], sems.at[i]).start()
        return 0

    lax.fori_loop(0, 8, block, 0)

    def done(i, _):
        pltpu.make_async_copy(stage.at[i], out.at[i], sems.at[i]).wait()
        return 0

    lax.fori_loop(0, 8, done, 0)


def body(state, gates):
    rows = state.reshape(2, 4096, 128).transpose(1, 0, 2).reshape(8, 1024, 128)
    f32 = jnp.float32
    landed = pl.pallas_call(
        evolve,
        out_shape=jax.ShapeDtypeStruct((2, HALF, 128), f32),
        in_specs=[pl.BlockSpec(memory_space=pl.ANY), pl.BlockSpec(memory_space=pltpu.HBM)],
        out_specs=pl.BlockSpec(memory_space=pl.ANY),
        scratch_shapes=[
            pltpu.VMEM((8, 1024, 128), f32),
            pltpu.VMEM((8192 + 64, 128), f32),
            pltpu.VMEM((2, HALF, 128), f32),
            pltpu.VMEM((2, HALF, 128), f32),
            pltpu.VMEM((HALF + CHUNK, 128), f32),
            pltpu.VMEM((HALF + CHUNK, 128), f32),
            pltpu.VMEM((2, HALF + CHUNK, 128), f32),
            pltpu.VMEM((3, 2, 2, 64, 64), f32),
            pltpu.VMEM((6, 256, 256), jnp.bfloat16),
            pltpu.SemaphoreType.DMA((2,)),
            pltpu.SemaphoreType.DMA((4,)),
            pltpu.SemaphoreType.DMA((4,)),
            pltpu.SemaphoreType.DMA((4,)),
        ],
        compiler_params=pltpu.CompilerParams(
            collective_id=0, has_side_effects=True, vmem_limit_bytes=VMEM
        ),
        name="evolve",
    )(rows, pltpu.with_memory_space_constraint(gates, pltpu.HBM))
    shape = (8, 2, 8, 2, CHUNK, 128)
    out = pl.pallas_call(
        finish,
        out_shape=jax.ShapeDtypeStruct(shape, f32),
        in_specs=[pl.BlockSpec(memory_space=pltpu.VMEM)],
        out_specs=pl.BlockSpec(memory_space=pl.ANY),
        scratch_shapes=[pltpu.VMEM(shape, f32), pltpu.SemaphoreType.DMA((8,))],
        compiler_params=pltpu.CompilerParams(vmem_limit_bytes=16 * 2**20),
        name="finish",
    )(landed.reshape(2, 128, CHUNK, 128))
    return out.reshape(4096, 2, 128).transpose(1, 0, 2).reshape(2, -1)


def solution(mesh):
    placed = (P(None, ("qa", "qb")), P())
    return jax.shard_map(
        body, mesh=mesh, in_specs=placed, out_specs=P(None, ("qa", "qb")), check_vma=False
    )
```
